32 devices in a mesh: face: 4 (over x, core), tile: 2 (over y), dp: 4 (over z).
Axes of the slice: x: 2, y: 2, z: 4, core: 2. Of those that a mesh axis runs over, the one named last changes fastest.
Arguments:
- inputs: bfloat16 [4, 8, 32, 32, 128], P('dp', ('face', 'tile')), may hold values from -6 to 6
- weight: bfloat16 [9, 128, 128], replicated, may hold values from -0.1875 to 0.1875
- bias: float32 [128], replicated, may hold values from -3 to 3
- seam: int32 [6, 4, 3], replicated, may hold values from 0 to 5, as said below
- station_grad: bfloat16 [4, 1024, 128], P('dp', ('face', 'tile')), may hold values from -6 to 6
- station_tile: int32 [1024, 1], P(('face', 'tile')), may hold values from 0 to 5; in each aligned block of 128 rows (0 to 127, 128 to 255, ...) at most 42 rows name the same one
- station_cell: int32 [1024], P(('face', 'tile')), may hold values from 0 to 1023
Outputs:
- forward: bfloat16 [4, 8, 32, 32, 128], P('dp', ('face', 'tile'))
- input_grad: bfloat16 [4, 8, 32, 32, 128], P('dp', ('face', 'tile'))
- weight_grad: float32 [9, 128, 128], replicated
- bias_grad: float32 [128], replicated
The draws below stay inside these ranges and needn't reach their ends.
Inputs may be any that keep to these rules, and one draw needn't show every extreme that they name: seam glues the 6 panels as the faces of a cube: seam[q, e] = (q2, e2, f) glues side e of panel q to side e2 of panel q2, reversed if f = 1; then seam[q2, e2] = (q, e, f); no panel is glued to itself. Entries 0 and 1 name panels and sides, entry 2 is 0 or 1. `station_tile`: among the 128 stations of one device (aligned blocks of the list), at most 42 lie in any one tile.
All inputs are finite; a program needn't handle non-finite values.
Results may differ from the reference program's by a relative error of at most 0.006.
Values may be sent and summed in bfloat16 or wider, within the bound.
A program may use at most 64 MiB of HBM per device.

```python
import math
import jax
import jax.numpy as jnp
import numpy as np
from jax import lax

C = 128
S = 32
ST_DEV = 128
PANELS = 6
GRID = 1
TILES = 6
SLOTS = 8
BATCH = 4
STATIONS = 1024
CAP = 42


def draw_seam(key, part):
    glued = [[0, 0, 4, 1, 0], [0, 1, 5, 0, 0], [0, 3, 1, 2, 0], [1, 3, 2, 2, 0], [2, 3, 3, 2, 0], [3, 3, 0, 2, 0], [4, 3, 1, 0, 1], [4, 0, 2, 0, 1], [4, 2, 3, 0, 0], [5, 3, 1, 1, 0], [5, 1, 2, 1, 1], [5, 2, 3, 1, 1]]
    pairs = jnp.array(glued, jnp.int32)
    relabel = jax.random.permutation(key, PANELS).astype(jnp.int32)
    first_panel = relabel[pairs[:, 0]]
    second_panel = relabel[pairs[:, 2]]
    table = jnp.zeros((PANELS, 4, 3), jnp.int32)
    table = table.at[first_panel, pairs[:, 1]].set(jnp.stack([second_panel, pairs[:, 3], pairs[:, 4]], axis=1))
    table = table.at[second_panel, pairs[:, 3]].set(jnp.stack([first_panel, pairs[:, 1], pairs[:, 4]], axis=1))
    return table


def with_ends(values, own_key, least, top_value):
    longest = values.shape.index(max(values.shape))
    spots = []
    for shift in (0, 1):
        where = [jax.random.randint(jax.random.fold_in(own_key, axis), (), 0, length) for axis, length in enumerate(values.shape)]
        where[longest] = (where[longest] + shift) % values.shape[longest]
        spots.append(tuple(where))
    return values.at[spots[0]].set(least).at[spots[1]].set(top_value)


def levels(stream_key, shape, shards, least, top_value):
    level = 1.0
    for position, parts in shards:
        steps = jax.random.uniform(jax.random.fold_in(jax.random.fold_in(stream_key, 6), position), (parts,), jnp.float32, least / len(shards), top_value / len(shards))
        level = level * jnp.repeat(jnp.exp(steps), shape[position] // parts).reshape((-1,) + (1,) * (len(shape) - 1 - position))
    return level


def assign_block(rng, own, number, rows, amount, top, bound, skew):
    sequence = jax.random.permutation(rng, amount)
    heavy_load, usual = portions_of(amount, rows * top, bound, skew, True), portions_of(amount, rows * top, bound, skew, False)
    places = jnp.arange(amount)

    def named(tallies, turn):
        used = int((tallies > 0).sum())
        fixed = max(1, used // 4)
        passed = fixed + (places - fixed + turn * (used - fixed)) % max(1, amount - fixed)
        return jnp.zeros((amount,), jnp.int32).at[sequence[jnp.where(places < fixed, places, passed)]].set(jnp.asarray(tallies, jnp.int32))

    tallies = jnp.where(number % 4 == 0, named(heavy_load, number // 4), named(usual, number - number // 4 - 1))
    mixed = jax.random.permutation(jax.random.fold_in(own, 3), amount)
    source_of, receiver = mixed[0:amount // 2 * 2:2], mixed[1:amount // 2 * 2:2]
    slack = jnp.minimum(tallies[source_of] - 1, bound - tallies[receiver]) // 2
    slack = jnp.where((source_of == sequence[0]) | (receiver == sequence[0]) | (tallies[receiver] == 0), 0, jnp.maximum(slack, 0))
    passed = jax.random.randint(jax.random.fold_in(own, 4), (amount // 2,), 0, 1 << 20) % (slack + 1)
    tallies = tallies.at[source_of].add(-passed).at[receiver].add(passed)
    items = jnp.searchsorted(jnp.cumsum(tallies), jnp.arange(rows * top), side="right").astype(jnp.int32)
    table = items.reshape(top, rows).T
    table = table[jax.random.permutation(jax.random.fold_in(own, 1), rows)]
    turn = jax.random.randint(jax.random.fold_in(own, 2), (rows, 1), 0, top)
    return jnp.take_along_axis(table, (jnp.arange(top)[None, :] + turn) % top, axis=1)


def portions_of(count, total, limit, slope, full):
    loads = [(1 << 20) // math.isqrt(standing ** slope) + 1 for standing in range(1, count + 1)]
    largest = limit if full else min(limit, max(-(-total // count), total * loads[0] // sum(loads)))
    least = 1 if total - largest >= count - 1 else 0
    counts, spare = [largest] + [least] * (count - 1), total - largest - least * (count - 1)
    while spare > 0:
        candidates = [i for i in range(1, count) if counts[i] < largest] or [i for i in range(1, count) if counts[i] < limit]
        whole, budget = sum([loads[i] for i in candidates]), spare
        for i in candidates:
            addition = min(limit - counts[i], max(1, budget * loads[i] // whole), spare)
            counts[i] = counts[i] + addition
            spare = spare - addition
    return np.array(counts)


def centred(stream_key, dims, scale, bound, cuts=(), kind=jnp.bfloat16):
    gain = levels(stream_key, dims, cuts, -0.22, 0.18) if cuts else 1.0
    values = jax.random.normal(stream_key, dims, jnp.float32) * scale * gain
    return jnp.minimum(jnp.maximum(values, -bound), bound).astype(kind)


def setup_inputs(seed: int = 0) -> dict:
    key_of = jax.random.split(jax.random.key(seed), 8)
    inputs = centred(key_of[0], (BATCH, SLOTS, S, S, C), 1.0, 6.0, ((0, 4), (1, 8)))
    weight = centred(key_of[1], (9, C, C), (9 * C) ** -0.5, 0.1875)
    bias = centred(key_of[2], (C,), 0.5, 3.0, (), jnp.float32)
    seam = draw_seam(jax.random.fold_in(key_of[7], 71), 0)
    station_grad = centred(key_of[4], (BATCH, STATIONS, C), 1.0, 6.0, ((0, 4), (1, 8)))
    station_tile_keys = jax.random.split(jax.random.fold_in(key_of[5], 1), STATIONS // ST_DEV)
    station_tile_turns = jax.random.permutation(jax.random.fold_in(key_of[5], 3), STATIONS // ST_DEV)
    station_tile = jax.vmap(lambda own, number: assign_block(jax.random.fold_in(key_of[5], 2), own, number, ST_DEV, TILES, 1, CAP, 2))(station_tile_keys, station_tile_turns).reshape((STATIONS, 1))
    station_cell = with_ends(jax.random.randint(key_of[6], (STATIONS,), 0, S * S), jax.random.fold_in(key_of[6], 1), 0, (S * S) - 1).astype(jnp.int32)
    return dict(inputs=inputs, weight=weight, bias=bias, seam=seam, station_grad=station_grad, station_tile=station_tile, station_cell=station_cell)


def side_tables(tile_grid, panel_count):
    tables = []
    for side_id in range(4):
        rows_of = np.zeros((panel_count, tile_grid), np.int32)
        for panel in range(panel_count):
            for offset in range(tile_grid):
                if side_id == 0:
                    local = offset
                elif side_id == 1:
                    local = (tile_grid - 1) * tile_grid + offset
                elif side_id == 2:
                    local = offset * tile_grid
                else:
                    local = offset * tile_grid + tile_grid - 1
                rows_of[panel, offset] = panel * tile_grid * tile_grid + local
        tables.append(rows_of)
    return tables

def seam_pad(field, seam):
    count, extent, channels = (field.shape[0], field.shape[1], field.shape[3])
    tile_grid = GRID
    tile_count = tile_grid * tile_grid
    panel_count = count // tile_count
    strips = jnp.stack([field[:, 0], field[:, -1], field[:, :, 0], field[:, :, -1]], axis=1)
    tile_ids = np.arange(count)
    panel_of = tile_ids // tile_count
    tile_row = tile_ids % tile_count // tile_grid
    tile_col = tile_ids % tile_grid
    tables = side_tables(tile_grid, panel_count)
    side_lines = jnp.stack([strips[tables[s], s].reshape(panel_count, tile_grid * extent, channels) for s in range(4)], axis=1)
    beside = [tile_ids - tile_grid, tile_ids + tile_grid, tile_ids - 1, tile_ids + 1]
    facing = [1, 0, 3, 2]
    border = [tile_row == 0, tile_row == tile_grid - 1, tile_col == 0, tile_col == tile_grid - 1]
    along = [tile_col, tile_col, tile_row, tile_row]
    rims = []
    for side_id in range(4):
        inside = strips[np.clip(beside[side_id], 0, count - 1), facing[side_id]]
        seam_row = seam[panel_of, side_id]
        side_line = side_lines[seam_row[:, 0], seam_row[:, 1]]
        side_line = jnp.where((seam_row[:, 2] == 1)[:, None, None], side_line[:, ::-1], side_line)
        segment = side_line.reshape(count, tile_grid, extent, channels)[tile_ids, along[side_id]]
        rims.append(jnp.where(border[side_id][:, None, None], segment, inside))
    padded = jnp.zeros((count, extent + 2, extent + 2, channels), field.dtype)
    padded = padded.at[:, 1:-1, 1:-1].set(field)
    padded = padded.at[:, 0, 1:-1].set(rims[0])
    padded = padded.at[:, -1, 1:-1].set(rims[1])
    padded = padded.at[:, 1:-1, 0].set(rims[2])
    padded = padded.at[:, 1:-1, -1].set(rims[3])
    return padded

def convolve(padded, kernel):
    return lax.conv_general_dilated(padded.astype(jnp.float32), kernel.astype(jnp.float32), (1, 1), 'VALID', dimension_numbers=('NHWC', 'HWIO', 'NHWC'))

def reference(inputs, weight, bias, seam, station_grad, station_tile, station_cell):
    channels = weight.shape[1]
    extent = inputs.shape[2]
    count = TILES
    kernel = weight.reshape(3, 3, channels, channels)
    flipped = jnp.transpose(kernel[::-1, ::-1], (0, 1, 3, 2))
    flat_ids = (station_tile[:, 0] * (extent * extent) + station_cell).astype(jnp.int32)
    real_inputs = inputs[:, :count]

    def one_sample(packed):
        field, values = packed
        padded = seam_pad(field, seam)
        preact = convolve(padded, kernel) + bias
        output = (preact * jax.nn.sigmoid(preact)).astype(jnp.bfloat16)
        grad_out = jnp.zeros((count * extent * extent, channels), jnp.float32).at[flat_ids].add(values.astype(jnp.float32))
        grad_out = grad_out.reshape(count, extent, extent, channels)
        gating = jax.nn.sigmoid(preact)
        grad_pre = (grad_out * gating * (1.0 + preact * (1.0 - gating))).astype(jnp.bfloat16)
        grad_in = convolve(seam_pad(grad_pre, seam), flipped).astype(jnp.bfloat16)
        grad_wide = grad_pre.astype(jnp.float32)
        taps = []
        for tap_row in range(3):
            for tap_col in range(3):
                window = padded[:, tap_row:tap_row + extent, tap_col:tap_col + extent].astype(jnp.float32)
                taps.append(jnp.einsum('nijc,nijo->co', window, grad_wide))
        grad_weight = jnp.stack(taps, axis=0)
        grad_bias = lax.optimization_barrier(jnp.sum(grad_wide, axis=(0, 1, 2)))
        return (output, grad_in, grad_weight, grad_bias)
    outputs, grads_in, grads_weight, grads_bias = lax.map(one_sample, (real_inputs, station_grad))
    spare = jnp.zeros((inputs.shape[0], inputs.shape[1] - count, extent, extent, channels), jnp.bfloat16)
    outputs = jnp.concatenate([outputs, spare], axis=1)
    grads_in = jnp.concatenate([grads_in, spare], axis=1)
    factor = 1.0 / math.sqrt(BATCH * STATIONS)
    return (outputs, grads_in, lax.optimization_barrier(jnp.sum(grads_weight, axis=0)) * factor, lax.optimization_barrier(jnp.sum(grads_bias, axis=0)) * factor)
```

```python
import math

import jax
import jax.numpy as jnp
from jax import lax
from jax.sharding import PartitionSpec as P

GROUP = ("face", "tile")


def edge_strips(field):
    return jnp.stack([field[0], field[-1], field[:, 0], field[:, -1]], axis=0)


def rim_sources(seam):
    tiles_here = lax.axis_size("tile")
    grid = math.isqrt(tiles_here // 2)
    count = grid * grid
    slot = jnp.minimum(lax.axis_index(GROUP), seam.shape[0] * count - 1)
    panel, local = slot // count, slot % count
    row, col = local // grid, local % grid
    border = [row == 0, row == grid - 1, col == 0, col == grid - 1]
    steps, facing, along = [-grid, grid, -1, 1], [1, 0, 3, 2], [col, col, row, row]
    out = []
    for e in range(4):
        q, side, flag = seam[panel, e, 0], seam[panel, e, 1], seam[panel, e, 2]
        k = jnp.where(flag == 1, grid - 1 - along[e], along[e])
        far = jnp.where(
            side == 0, k, jnp.where(side == 1, (grid - 1) * grid + k,
                                    jnp.where(side == 2, k * grid, k * grid + grid - 1)))
        out.append((
            jnp.where(border[e], q * count + far, slot + steps[e]),
            jnp.where(border[e], side, facing[e]),
            border[e] & (flag == 1),
        ))
    return out


def pad(field, gathered, sources):
    rims = []
    for slot, side, flip in sources:
        strip = lax.dynamic_slice(
            gathered, (slot, side, 0, 0), (1, 1) + gathered.shape[2:])[0, 0]
        rims.append(jnp.where(flip, strip[::-1], strip))
    zero = jnp.zeros((1, field.shape[2]), field.dtype)
    middle = jnp.concatenate([rims[2][:, None], field, rims[3][:, None]], axis=1)
    top = jnp.concatenate([zero, rims[0], zero], axis=0)[None]
    bottom = jnp.concatenate([zero, rims[1], zero], axis=0)[None]
    return jnp.concatenate([top, middle, bottom], axis=0)


def patches(padded):
    s = padded.shape[0] - 2
    return jnp.concatenate(
        [padded[a : a + s, b : b + s] for a in range(3) for b in range(3)], axis=-1
    ).reshape(s * s, -1)


def body(inputs, weight, bias, seam, station_grad, station_tile, station_cell):
    field = inputs[0, 0]
    s, c = field.shape[0], field.shape[2]
    grid = math.isqrt(lax.axis_size("tile") // 2)
    slots = lax.axis_size(GROUP)
    stations = station_cell.shape[0]
    me = lax.axis_index(GROUP)
    active = me < seam.shape[0] * grid * grid
    sources = rim_sources(seam)

    sent = jnp.concatenate([edge_strips(field).reshape(4 * s, c), station_grad[0]], axis=0)
    got = lax.all_gather(sent, GROUP, axis=0)
    key = station_tile[:, 0] * (s * s) + station_cell
    keys = lax.all_gather(key, GROUP, axis=0, tiled=True)
    lines = got[:, : 4 * s].reshape(slots, 4, s, c)
    values = got[:, 4 * s :].reshape(slots * stations, c)

    cols = patches(pad(field, lines, sources))
    preact = jnp.dot(cols, weight.reshape(9 * c, c), preferred_element_type=jnp.float32) + bias
    gate = jax.nn.sigmoid(preact)
    output = jnp.where(active, preact * gate, 0.0).astype(jnp.bfloat16).reshape(field.shape)

    cells = me * (s * s) + lax.broadcasted_iota(jnp.int32, (s * s, 1), 0)
    hits = (cells == keys[None, :]).astype(jnp.bfloat16)
    grad_out = jnp.dot(hits, values, preferred_element_type=jnp.float32)
    grad_pre = (grad_out * gate * (1.0 + preact * (1.0 - gate))).astype(jnp.bfloat16)

    grad_field = grad_pre.reshape(field.shape)
    edges = lax.all_gather(edge_strips(grad_field), GROUP, axis=0)
    flipped = jnp.transpose(weight[::-1], (0, 2, 1)).reshape(9 * c, c)
    grad_in = jnp.dot(
        patches(pad(grad_field, edges, sources)), flipped, preferred_element_type=jnp.float32)
    grad_in = jnp.where(active, grad_in, 0.0).astype(jnp.bfloat16).reshape(field.shape)

    grad_w = lax.dot_general(
        cols, grad_pre, (((0,), (0,)), ((), ())), preferred_element_type=jnp.float32)
    grad_b = jnp.sum(grad_pre.astype(jnp.float32), axis=0, keepdims=True)
    terms = jnp.concatenate([grad_w, jnp.broadcast_to(grad_b, (8, c))], axis=0)
    terms = jnp.where(active, terms, 0.0)
    total = lax.psum(terms, ("face", "tile", "dp"))
    total = total / math.sqrt(lax.axis_size("dp") * slots * stations)
    return (output[None, None], grad_in[None, None],
            total[: 9 * c].reshape(9, c, c), total[9 * c])


def solution(mesh):
    return jax.shard_map(
        body,
        mesh=mesh,
        in_specs=(
            P("dp", GROUP, None, None, None),
            P(),
            P(),
            P(),
            P("dp", GROUP, None),
            P(GROUP, None),
            P(GROUP),
        ),
        out_specs=(
            P("dp", GROUP, None, None, None),
            P("dp", GROUP, None, None, None),
            P(),
            P(),
        ),
        check_vma=False,
    )
```

```python
import math

import jax
import jax.numpy as jnp
from jax import lax
from jax.sharding import PartitionSpec as P

GROUP = ("face", "tile")


def edge_strips(field):
    return jnp.stack([field[0], field[-1], field[:, 0], field[:, -1]], axis=0)


def rim_sources(seam):
    tiles_here = lax.axis_size("tile")
    grid = math.isqrt(tiles_here // 2)
    count = grid * grid
    slot = jnp.minimum(lax.axis_index(GROUP), seam.shape[0] * count - 1)
    panel, local = slot // count, slot % count
    row, col = local // grid, local % grid
    border = [row == 0, row == grid - 1, col == 0, col == grid - 1]
    steps, facing, along = [-grid, grid, -1, 1], [1, 0, 3, 2], [col, col, row, row]
    out = []
    for e in range(4):
        q, side, flag = seam[panel, e, 0], seam[panel, e, 1], seam[panel, e, 2]
        k = jnp.where(flag == 1, grid - 1 - along[e], along[e])
        far = jnp.where(
            side == 0, k, jnp.where(side == 1, (grid - 1) * grid + k,
                                    jnp.where(side == 2, k * grid, k * grid + grid - 1)))
        out.append((
            jnp.where(border[e], q * count + far, slot + steps[e]),
            jnp.where(border[e], side, facing[e]),
            border[e] & (flag == 1),
        ))
    return out


def pad(field, gathered, sources):
    rims = []
    for slot, side, flip in sources:
        strip = lax.dynamic_slice(
            gathered, (slot, side, 0, 0), (1, 1) + gathered.shape[2:])[0, 0]
        rims.append(jnp.where(flip, strip[::-1], strip))
    zero = jnp.zeros((1, field.shape[2]), field.dtype)
    middle = jnp.concatenate([rims[2][:, None], field, rims[3][:, None]], axis=1)
    top = jnp.concatenate([zero, rims[0], zero], axis=0)[None]
    bottom = jnp.concatenate([zero, rims[1], zero], axis=0)[None]
    return jnp.concatenate([top, middle, bottom], axis=0)


def patches(padded):
    s = padded.shape[0] - 2
    return jnp.concatenate(
        [padded[a : a + s, b : b + s] for a in range(3) for b in range(3)], axis=-1
    ).reshape(s * s, -1)


def body(inputs, weight, bias, seam, station_grad, station_tile, station_cell):
    field = inputs[0, 0]
    s, c = field.shape[0], field.shape[2]
    grid = math.isqrt(lax.axis_size("tile") // 2)
    slots = lax.axis_size(GROUP)
    stations = station_cell.shape[0]
    me = lax.axis_index(GROUP)
    active = me < seam.shape[0] * grid * grid
    sources = rim_sources(seam)

    places = jnp.stack([station_tile[:, 0], station_cell // s, station_cell % s])
    places = jnp.pad(places.reshape(-1, c), ((0, 16 - 3 * stations // c), (0, 0)))
    sent = jnp.concatenate(
        [edge_strips(field).reshape(4 * s, c), station_grad[0], places.astype(jnp.bfloat16)], axis=0)
    got = lax.all_gather(sent, GROUP, axis=0)
    lines = got[:, : 4 * s].reshape(slots, 4, s, c)
    values = got[:, 4 * s : 4 * s + stations].reshape(slots * stations, c)
    places = got[:, 4 * s + stations :].astype(jnp.int32).reshape(slots, -1)
    part = [places[:, i * stations : (i + 1) * stations] for i in range(3)]
    keys = (part[0] * (s * s) + part[1] * s + part[2]).reshape(-1)

    cols = patches(pad(field, lines, sources))
    preact = jnp.dot(cols, weight.reshape(9 * c, c), preferred_element_type=jnp.float32) + bias
    gate = jax.nn.sigmoid(preact)
    output = jnp.where(active, preact * gate, 0.0).astype(jnp.bfloat16).reshape(field.shape)

    cells = me * (s * s) + lax.broadcasted_iota(jnp.int32, (s * s, 1), 0)
    hits = (cells == keys[None, :]).astype(jnp.bfloat16)
    grad_out = jnp.dot(hits, values, preferred_element_type=jnp.float32)
    grad_pre = (grad_out * gate * (1.0 + preact * (1.0 - gate))).astype(jnp.bfloat16)

    grad_field = grad_pre.reshape(field.shape)
    edges = lax.all_gather(edge_strips(grad_field), GROUP, axis=0)
    flipped = jnp.transpose(weight[::-1], (0, 2, 1)).reshape(9 * c, c)
    grad_in = jnp.dot(
        patches(pad(grad_field, edges, sources)), flipped, preferred_element_type=jnp.float32)
    grad_in = jnp.where(active, grad_in, 0.0).astype(jnp.bfloat16).reshape(field.shape)

    grad_w = lax.dot_general(
        cols, grad_pre, (((0,), (0,)), ((), ())), preferred_element_type=jnp.float32)
    grad_b = jnp.sum(grad_pre.astype(jnp.float32), axis=0, keepdims=True)
    everyone = ("face", "tile", "dp")
    devices = lax.axis_size(everyone)
    rows = -(-(9 * c + 1) // (8 * devices)) * 8
    terms = jnp.concatenate([grad_w, grad_b], axis=0)
    terms = jnp.where(active, terms, 0.0).astype(jnp.bfloat16)
    terms = jnp.pad(terms, ((0, rows * devices - terms.shape[0]), (0, 0)))
    shares = lax.all_to_all(terms.reshape(devices, rows, c), everyone, 0, 0)
    share = jnp.sum(shares.astype(jnp.float32), axis=0)
    share = share / math.sqrt(lax.axis_size("dp") * slots * stations)
    total = lax.all_gather(share.astype(jnp.bfloat16), everyone, axis=0, tiled=True)
    total = total.astype(jnp.float32)
    return (output[None, None], grad_in[None, None],
            total[: 9 * c].reshape(9, c, c), total[9 * c])


def solution(mesh):
    return jax.shard_map(
        body,
        mesh=mesh,
        in_specs=(
            P("dp", GROUP, None, None, None),
            P(),
            P(),
            P(),
            P("dp", GROUP, None),
            P(GROUP, None),
            P(GROUP),
        ),
        out_specs=(
            P("dp", GROUP, None, None, None),
            P("dp", GROUP, None, None, None),
            P(),
            P(),
        ),
        check_vma=False,
    )
```
